32 devices in a mesh: groups: 2 (over y), sec: 16 (over z, x, core).
Axes of the slice: x: 2, y: 2, z: 4, core: 2. Of those that a mesh axis runs over, the one named last changes fastest.
Arguments:
- psi: bfloat16 [4096, 64, 128], P(('groups', 'sec')), parts along dimension 0, may hold values from -6 to 6
- block_rows: int32 [4096], P(('groups', 'sec')), parts along dimension 0, may hold values from 1 to 64, as said below
- owner: int32 [4096, 1], P(('groups', 'sec')), parts along dimension 0, may hold values from 0 to 15; in each aligned block of 128 rows (0 to 127, 128 to 255, ...) at most 16 rows name the same one
- left_sector: int32 [4096], P(('groups', 'sec')), parts along dimension 0, may hold values from 0 to 3
- right_sector: int32 [4096], P(('groups', 'sec')), parts along dimension 0, may hold values from 0 to 31
- left_env: bfloat16 [128, 3, 64, 64], P(('groups', 'sec')), parts along dimension 0, may hold values from -0.75 to 0.75
- right_env: bfloat16 [1024, 2, 128, 128], P(('groups', 'sec')), parts along dimension 0, may hold values from -0.5 to 0.5
Outputs:
- h_psi: bfloat16 [4096, 64, 128], P(('groups', 'sec')), parts along dimension 0
The draws below stay inside these ranges and needn't reach their ends.
There are 2 independent parts, one for each index of `groups`. The reference program is written for one: setup_inputs(seed, part) draws one part's arguments, and reference() takes and returns one part's arrays. A program takes and returns all parts, laid end to end along the dimension named above; each array names one. Nothing has to cross between parts.
Inputs may be any that keep to these rules, and one draw needn't show every extreme that they name: `block_rows`: the first block of the part has a full left sector of 64 rows. Among the blocks of one device, at most 16 name the same owner, a bound that some block reaches.
All inputs are finite; a program needn't handle non-finite values.
Results may differ from the reference program's by a relative error of at most 0.0043.
Values may be sent and summed in bfloat16 or wider, within the bound.
A program may use at most 128 MiB of HBM per device.

```python
import math
import jax
import jax.numpy as jnp
import numpy as np
from jax import lax

BL = 64
BR = 128
KTERMS = 2
BLK = 128
LSEC = 4
CAP = 16
RSEC = 32
NBLOCKS = 2048
N_SEC = 16


def draw_block_rows(key, part):
    key = jax.random.fold_in(key, 7)
    sizes = jax.random.randint(key, (NBLOCKS,), 1, BL + 1, dtype=jnp.int32)
    return sizes.at[0].set(BL)


def with_ends(result, key, least, top_value):
    spot = [jax.random.randint(jax.random.fold_in(key, axis), (), 0, length) for axis, length in enumerate(result.shape)]
    longest = result.shape.index(max(result.shape))
    neighbour = spot[:longest] + [(spot[longest] + 1) % result.shape[longest]] + spot[longest + 1:]
    return result.at[tuple(spot)].set(least).at[tuple(neighbour)].set(top_value)


def block_scale(key, extent, split, low, largest):
    gain = 1.0
    for dim, blocks in split:
        steps = jax.random.uniform(jax.random.fold_in(jax.random.fold_in(key, 6), dim), (blocks,), jnp.float32, low / len(split), largest / len(split))
        gain = gain * jnp.repeat(jnp.exp(steps), extent[dim] // blocks).reshape((-1,) + (1,) * (len(extent) - 1 - dim))
    return gain


def routed_block(key, own, number, rows, number_of, top, reach, skew):
    order = jax.random.permutation(key, number_of)
    packed, usual = load_shares(number_of, rows * top, reach, skew, True), load_shares(number_of, rows * top, reach, skew, False)
    places = jnp.arange(number_of)

    def named(lengths, offset_by):
        used = int((lengths > 0).sum())
        fixed = max(1, used // 4)
        passed = fixed + (places - fixed + offset_by * (used - fixed)) % max(1, number_of - fixed)
        return jnp.zeros((number_of,), jnp.int32).at[order[jnp.where(places < fixed, places, passed)]].set(jnp.asarray(lengths, jnp.int32))

    lengths = jnp.where(number % 4 == 0, named(packed, number // 4), named(usual, number - number // 4 - 1))
    mixed = jax.random.permutation(jax.random.fold_in(own, 3), number_of)
    donor, taker = mixed[0:number_of // 2 * 2:2], mixed[1:number_of // 2 * 2:2]
    slack = jnp.minimum(lengths[donor] - 1, reach - lengths[taker]) // 2
    slack = jnp.where((donor == order[0]) | (taker == order[0]) | (lengths[taker] == 0), 0, jnp.maximum(slack, 0))
    passed = jax.random.randint(jax.random.fold_in(own, 4), (number_of // 2,), 0, 1 << 20) % (slack + 1)
    lengths = lengths.at[donor].add(-passed).at[taker].add(passed)
    members = jnp.searchsorted(jnp.cumsum(lengths), jnp.arange(rows * top), side="right").astype(jnp.int32)
    listing = members.reshape(top, rows).T
    listing = listing[jax.random.permutation(jax.random.fold_in(own, 1), rows)]
    offset_by = jax.random.randint(jax.random.fold_in(own, 2), (rows, 1), 0, top)
    return jnp.take_along_axis(listing, (jnp.arange(top)[None, :] + offset_by) % top, axis=1)


def load_shares(amount, total, most, slope, full):
    portions = [(1 << 20) // math.isqrt(grade ** slope) + 1 for grade in range(1, amount + 1)]
    largest = most if full else min(most, max(-(-total // amount), total * portions[0] // sum(portions)))
    least = 1 if total - largest >= amount - 1 else 0
    holding, rest = [largest] + [least] * (amount - 1), total - largest - least * (amount - 1)
    while rest > 0:
        candidates = [i for i in range(1, amount) if holding[i] < largest] or [i for i in range(1, amount) if holding[i] < most]
        whole, remaining = sum([portions[i] for i in candidates]), rest
        for i in candidates:
            more = min(most - holding[i], max(1, remaining * portions[i] // whole), rest)
            holding[i] = holding[i] + more
            rest = rest - more
    return np.array(holding)


def centred(rng, dims, width, limit, cuts=(), held_as=jnp.bfloat16):
    values = jax.random.normal(rng, dims, jnp.float32) * width
    if len(cuts) > 0:
        values = block_scale(rng, dims, cuts, -0.22, 0.18) * values
    return jnp.clip(values, min=-limit, max=limit).astype(held_as)


def setup_inputs(seed: int = 0, part: int = 0) -> dict:
    streams_of = jax.random.split(jax.random.key(seed), 8)
    part_splits = jax.random.split(jax.random.fold_in(streams_of[7], part), 8)
    psi = centred(part_splits[0], (NBLOCKS, BL, BR), 1.0, 6.0, ((0, 16),))
    block_rows = draw_block_rows(jax.random.fold_in(jax.random.fold_in(streams_of[7], part), 71), part)
    owner_keys = jax.random.split(jax.random.fold_in(part_splits[2], 1), NBLOCKS // BLK)
    owner_turns = jax.random.permutation(jax.random.fold_in(part_splits[2], 3), NBLOCKS // BLK)
    owner = jax.vmap(lambda own, number: routed_block(jax.random.fold_in(part_splits[2], 2), own, number, BLK, N_SEC, 1, CAP, 2))(owner_keys, owner_turns).reshape((NBLOCKS, 1))
    left_sector = with_ends(jax.random.randint(part_splits[3], (NBLOCKS,), 0, LSEC), jax.random.fold_in(part_splits[3], 1), 0, LSEC - 1).astype(jnp.int32)
    right_sector = with_ends(jax.random.randint(part_splits[4], (NBLOCKS,), 0, RSEC), jax.random.fold_in(part_splits[4], 1), 0, RSEC - 1).astype(jnp.int32)
    left_env = centred(part_splits[5], (N_SEC * LSEC, KTERMS + 1, BL, BL), BL ** -0.5, 0.75, ((0, 16),))
    right_env = centred(part_splits[6], (N_SEC * RSEC, KTERMS, BR, BR), BR ** -0.5, 0.5, ((0, 16),))
    return dict(psi=psi, block_rows=block_rows, owner=owner, left_sector=left_sector, right_sector=right_sector, left_env=left_env, right_env=right_env)


def reference(psi, block_rows, owner, left_sector, right_sector, left_env, right_env):
    total = psi.shape[0]
    valid = jnp.arange(BL, dtype=jnp.int32)[None, :] < block_rows[:, None]
    masked = jnp.where(valid[:, :, None], psi, jnp.zeros((), psi.dtype))
    home = jnp.arange(total, dtype=jnp.int32) // BLK
    left_index = (home * LSEC + left_sector).astype(jnp.int32)
    right_index = (owner[:, 0] * RSEC + right_sector).astype(jnp.int32)

    def device_blocks(dev):
        start = (dev * BLK).astype(jnp.int32)
        piece = lax.dynamic_slice_in_dim(masked, start, BLK, 0).astype(jnp.float32)
        lrow = lax.dynamic_slice_in_dim(left_index, start, BLK, 0)
        rrow = lax.dynamic_slice_in_dim(right_index, start, BLK, 0)
        keep = lax.dynamic_slice_in_dim(valid, start, BLK, 0)
        lenv = left_env[lrow].astype(jnp.float32)
        renv = right_env[rrow].astype(jnp.float32)
        local = jnp.einsum('bij,bjc->bic', lenv[:, 0], piece)
        moved = jnp.einsum('bkij,bjc->bkic', lenv[:, 1:], piece).astype(jnp.bfloat16)
        moved = lax.optimization_barrier(moved).astype(jnp.float32)
        far = jnp.einsum('bkic,bkcl->bil', moved, renv)
        return jnp.where(keep[:, :, None], local + far, jnp.float32(0.0)).astype(jnp.bfloat16)

    out = lax.map(device_blocks, jnp.arange(N_SEC, dtype=jnp.int32))
    return out.reshape(total, BL, BR)
```

```python
import functools

import jax
import jax.numpy as jnp
from jax import lax
from jax.experimental import pallas as pl
from jax.experimental.pallas import tpu as pltpu
from jax.sharding import PartitionSpec as P


def apply_kernel(step, cap, lsec, terms, lsel, rsel, rows, psi_ref, left_ref, right_ref, out_ref):
    bl, br = psi_ref.shape[1:]
    line = lax.broadcasted_iota(jnp.int32, (bl, br), 0)
    base = pl.program_id(0) * step
    for g in range(step):
        slot = base + g
        peer = slot // cap
        keep = line < rows[slot]
        block = jnp.where(keep, psi_ref[g], jnp.zeros((), psi_ref.dtype))
        left = left_ref[peer * lsec + lsel[slot]]
        made = jnp.dot(left, block, preferred_element_type=jnp.float32)
        moved = jnp.concatenate(
            [made[(k + 1) * bl:(k + 2) * bl].astype(jnp.bfloat16) for k in range(terms)], axis=1
        )
        far = jnp.dot(moved, right_ref[rsel[slot]], preferred_element_type=jnp.float32)
        out_ref[g] = jnp.where(keep, made[:bl] + far, jnp.float32(0.0)).astype(out_ref.dtype)


def apply_blocks(blocks, tags, left, right, peers, cap, lsec):
    slots, bl, br = blocks.shape
    rsec, terms = right.shape[:2]
    rows = tags % (bl + 1)
    lsel = (tags // (bl + 1)) % lsec
    rsel = tags // ((bl + 1) * lsec)
    step = 16
    left = left.reshape(peers * lsec, (terms + 1) * bl, bl)
    right = right.reshape(rsec, terms * br, br)
    return pl.pallas_call(
        functools.partial(apply_kernel, step, cap, lsec, terms),
        grid_spec=pltpu.PrefetchScalarGridSpec(
            num_scalar_prefetch=3,
            grid=(slots // step,),
            in_specs=[
                pl.BlockSpec((step, bl, br), lambda i, *_: (i, 0, 0)),
                pl.BlockSpec(left.shape, lambda i, *_: (0, 0, 0)),
                pl.BlockSpec(right.shape, lambda i, *_: (0, 0, 0)),
            ],
            out_specs=pl.BlockSpec((step, bl, br), lambda i, *_: (i, 0, 0)),
        ),
        out_shape=jax.ShapeDtypeStruct(blocks.shape, jnp.bfloat16),
        compiler_params=pltpu.CompilerParams(vmem_limit_bytes=40 * 1024 * 1024),
        cost_estimate=pl.CostEstimate(
            flops=2 * slots * bl * br * ((terms + 1) * bl + terms * br),
            bytes_accessed=4 * slots * bl * br + 2 * left.size + 2 * right.size,
            transcendentals=0,
        ),
    )(lsel, rsel, rows, blocks, left, right)


def shards(psi, block_rows, owner, left_sector, right_sector, left_env, right_env):
    blocks, bl, br = psi.shape
    n = lax.axis_size("sec")
    half = n // 2
    cap = max(2, 2 * blocks // n)
    lsec = left_env.shape[0]
    groups = [list(range(half)), list(range(half, n))]
    mirrored = lax.ppermute(right_env, "sec", [(i, (i + half) % n) for i in range(n)])

    exchange = functools.partial(
        lax.all_to_all, axis_name="sec", split_axis=0, concat_axis=0, axis_index_groups=groups, tiled=True
    )
    mine = lax.axis_index("sec") // half
    target = owner[:, 0]
    order = jnp.arange(blocks, dtype=jnp.int32)
    same = target[:, None] == target[None, :]
    earlier = order[None, :] < order[:, None]
    slot = jnp.sum(jnp.where(same & earlier, 1, 0), axis=1).astype(jnp.int32)
    kind = jnp.where(target // half == mine, 0, 1)
    spot = (target % half) * cap + slot
    position = kind * (half * cap) + spot
    slots_all = jnp.arange(n * cap, dtype=jnp.int32)
    match = position[None, :] == slots_all[:, None]
    tag = (right_sector * lsec + left_sector) * (bl + 1) + block_rows
    source = jnp.sum(jnp.where(match, order[None, :], 0), axis=1)
    tags = jnp.sum(jnp.where(match, tag[None, :], 0), axis=1)

    sent = [psi[source[k * half * cap:(k + 1) * half * cap]] for k in range(2)]
    tags = exchange(tags.reshape(2, half, cap).transpose(1, 0, 2)).transpose(1, 0, 2).reshape(2, half * cap)
    left = lax.all_gather(left_env, "sec", axis_index_groups=groups, tiled=True)
    returned = []
    for k, right in enumerate((right_env, mirrored)):
        arrived = exchange(sent[k].reshape(half, cap, bl, br)).reshape(half * cap, bl, br)
        done = apply_blocks(arrived, tags[k], left, right, half, cap, lsec)
        returned.append(exchange(done.reshape(half, cap, bl, br)).reshape(half * cap, bl, br))
    near = returned[0][jnp.where(kind == 0, spot, 0)]
    far = returned[1][jnp.where(kind == 0, 0, spot)]
    return jnp.where((kind == 0)[:, None, None], near, far)


def solution(mesh):
    return jax.shard_map(
        shards,
        mesh=mesh,
        in_specs=(
            P(("groups", "sec"), None, None),
            P(("groups", "sec")),
            P(("groups", "sec"), None),
            P(("groups", "sec")),
            P(("groups", "sec")),
            P(("groups", "sec"), None, None, None),
            P(("groups", "sec"), None, None, None),
        ),
        out_specs=P(("groups", "sec"), None, None),
        check_vma=False,
    )
```

```python
import functools

import jax
import jax.numpy as jnp
from jax import lax
from jax.experimental import pallas as pl
from jax.experimental.pallas import tpu as pltpu
from jax.sharding import PartitionSpec as P

F32 = jnp.float32


def route_kernel(
    n, lsec,
    source, position, tags_in, psi, left_in, right_in,
    out,
    sent, got, back, total, right, mirror0, mirror1, left, tags_v, tags,
    psi_send, psi_recv, ret_send, ret_recv, tag_send, tag_recv, left_send, left_recv,
    mir_send, mir_recv, own_sem, tag_sem,
):
    half = n // 2
    cap, bl, br = sent.shape[2:]
    me = lax.axis_index("sec")
    first = (me // half) * half
    mine = me - first
    partner = lax.rem(me + half, n)

    barrier = pltpu.get_barrier_semaphore()

    def greet(j, c):
        pl.semaphore_signal(barrier, inc=1, device_id={"sec": first + lax.rem(mine + j, half)})
        return c

    lax.fori_loop(1, half, greet, 0)
    pl.semaphore_signal(barrier, inc=1, device_id={"sec": partner})
    pl.semaphore_wait(barrier, half)

    mirrors = (mirror0, mirror1)

    def mirror_copy(k):
        return pltpu.make_async_remote_copy(
            src_ref=right_in.at[:, k], dst_ref=mirrors[k], send_sem=mir_send.at[k],
            recv_sem=mir_recv.at[k], device_id={"sec": partner},
        )

    def tag_copy(to, slot):
        return pltpu.make_async_remote_copy(
            src_ref=tags_in.at[to], dst_ref=tags_v.at[slot], send_sem=tag_send.at[to],
            recv_sem=tag_recv.at[slot], device_id={"sec": first + to},
        )

    def left_copy(to, slot):
        return pltpu.make_async_remote_copy(
            src_ref=left_in, dst_ref=left.at[slot], send_sem=left_send.at[to],
            recv_sem=left_recv.at[slot], device_id={"sec": first + to},
        )

    def psi_copy(kind, to, slot):
        return pltpu.make_async_remote_copy(
            src_ref=sent.at[kind, to], dst_ref=got.at[kind, slot], send_sem=psi_send.at[kind, to],
            recv_sem=psi_recv.at[kind, slot], device_id={"sec": first + to},
        )

    def ret_copy(kind, to, slot):
        return pltpu.make_async_remote_copy(
            src_ref=got.at[kind, to], dst_ref=back.at[kind, slot], send_sem=ret_send.at[kind, to],
            recv_sem=ret_recv.at[kind, slot], device_id={"sec": first + to},
        )

    mirror_copy(0).start()
    mirror_copy(1).start()
    own = [
        pltpu.make_async_copy(right_in, right, own_sem.at[0]),
        pltpu.make_async_copy(left_in, left.at[mine], own_sem.at[1]),
        pltpu.make_async_copy(tags_in.at[mine], tags_v.at[mine], own_sem.at[2]),
    ]
    for copy in own:
        copy.start()

    def send_small(j, c):
        to = lax.rem(mine + j, half)
        tag_copy(to, mine).start()
        left_copy(to, mine).start()
        return c

    lax.fori_loop(1, half, send_small, 0)

    def pack(kind, dest, into):
        def one(s, c):
            into[kind, dest, s] = psi[source[(kind * half + dest) * cap + s]]
            return c
        lax.fori_loop(0, cap, one, 0, unroll=min(cap, 4))

    for kind in range(2):
        def send_psi(j, c):
            to = lax.rem(mine + j, half)
            pack(kind, to, sent)
            psi_copy(kind, to, mine).start()
            return c
        lax.fori_loop(1, half, send_psi, 0)
        pack(kind, mine, got)

    for copy in own:
        copy.wait()

    def take_small(j, c):
        src = lax.rem(mine + half - j, half)
        tag_copy(src, src).wait_recv()
        left_copy(src, src).wait_recv()
        return c

    lax.fori_loop(1, half, take_small, 0)
    copy = pltpu.make_async_copy(tags_v, tags, tag_sem)
    copy.start()
    copy.wait()

    group = min(cap, 8)
    line = lax.broadcasted_iota(jnp.int32, (bl, br), 0)

    def fields(kind, src, s):
        tag = tags[src, 0, kind * cap + s]
        return tag % (bl + 1), (tag // (bl + 1)) % lsec, tag // ((bl + 1) * lsec)

    def contract_left(kind, src, s):
        rows, lsel, _ = fields(kind, src, s)
        block = jnp.where(line < rows, got[kind, src, s], jnp.zeros((), jnp.bfloat16))
        packed = left[src, lsel]
        made = jnp.concatenate([
            jnp.dot(packed[:, :bl], block, preferred_element_type=F32),
            jnp.dot(packed[:, bl:], block, preferred_element_type=F32),
        ], axis=0)
        return made[:bl], made[bl:2 * bl].astype(jnp.bfloat16), made[2 * bl:].astype(jnp.bfloat16)

    def over_groups(work):
        def one(g, c):
            work([g * group + i for i in range(group)])
            return c
        lax.fori_loop(0, cap // group, one, 0)

    def whole(kind, src, into):
        def work(slots):
            parts = [contract_left(kind, src, s) for s in slots]
            for s, (local, m0, m1) in zip(slots, parts):
                rows, _, rsel = fields(kind, src, s)
                far = jnp.dot(m0, right[rsel, 0], preferred_element_type=F32)
                far = far + jnp.dot(m1, right[rsel, 1], preferred_element_type=F32)
                into[kind, src, s] = jnp.where(line < rows, local + far, 0.0).astype(jnp.bfloat16)
        over_groups(work)

    def first_term(src):
        def work(slots):
            parts = [contract_left(1, src, s) for s in slots]
            for s, (local, m0, m1) in zip(slots, parts):
                _, _, rsel = fields(1, src, s)
                total[src, s] = local + jnp.dot(m0, mirror0[rsel], preferred_element_type=F32)
                got[1, src, s] = m1
        over_groups(work)

    def second_term(src, into):
        def work(slots):
            for s in slots:
                rows, _, rsel = fields(1, src, s)
                far = total[src, s] + jnp.dot(got[1, src, s], mirror1[rsel], preferred_element_type=F32)
                into[1, src, s] = jnp.where(line < rows, far, 0.0).astype(jnp.bfloat16)
        over_groups(work)

    def serve_near(j, c):
        src = lax.rem(mine + half - j, half)
        psi_copy(0, src, src).wait_recv()
        whole(0, src, got)
        ret_copy(0, src, mine).start()
        return c

    lax.fori_loop(1, half, serve_near, 0)
    whole(0, mine, back)

    mirror_copy(0).wait_recv()

    def begin_far(j, c):
        src = lax.rem(mine + half - j, half)
        psi_copy(1, src, src).wait_recv()
        first_term(src)
        return c

    lax.fori_loop(1, half, begin_far, 0)
    first_term(mine)

    mirror_copy(1).wait_recv()

    def end_far(j, c):
        src = lax.rem(mine + half - j, half)
        second_term(src, got)
        ret_copy(1, src, mine).start()
        return c

    lax.fori_loop(1, half, end_far, 0)
    second_term(mine, back)

    def take_back(j, c):
        src = lax.rem(mine + half - j, half)
        ret_copy(0, src, src).wait_recv()
        ret_copy(1, src, src).wait_recv()
        return c

    lax.fori_loop(1, half, take_back, 0)

    def unpack(i, c):
        p = position[i]
        out[i] = back[p // (half * cap), (p // cap) % half, p % cap]
        return c

    lax.fori_loop(0, out.shape[0], unpack, 0, unroll=4)

    def finish(j, c):
        to = lax.rem(mine + j, half)
        tag_copy(to, mine).wait_send()
        left_copy(to, mine).wait_send()
        for kind in range(2):
            psi_copy(kind, to, mine).wait_send()
            ret_copy(kind, to, mine).wait_send()
        return c

    lax.fori_loop(1, half, finish, 0)
    for k in range(2):
        mirror_copy(k).wait_send()


def route(source, position, tags, psi, left, right, n, cap, lsec):
    half = n // 2
    blocks, bl, br = psi.shape
    rsec = right.shape[0]
    slots = (2, half, cap, bl, br)
    vmem, smem = pl.BlockSpec(memory_space=pltpu.VMEM), pl.BlockSpec(memory_space=pltpu.SMEM)
    dma = pltpu.SemaphoreType.DMA
    return pl.pallas_call(
        functools.partial(route_kernel, n, lsec),
        out_shape=jax.ShapeDtypeStruct(psi.shape, jnp.bfloat16),
        in_specs=[smem, smem, vmem, vmem, vmem, pl.BlockSpec(memory_space=pl.ANY)],
        out_specs=vmem,
        scratch_shapes=[
            pltpu.VMEM(slots, jnp.bfloat16),
            pltpu.VMEM(slots, jnp.bfloat16),
            pltpu.VMEM(slots, jnp.bfloat16),
            pltpu.VMEM(slots[1:], F32),
            pltpu.VMEM(right.shape, jnp.bfloat16),
            pltpu.VMEM((rsec, br, br), jnp.bfloat16),
            pltpu.VMEM((rsec, br, br), jnp.bfloat16),
            pltpu.VMEM((half,) + left.shape, jnp.bfloat16),
            pltpu.VMEM(tags.shape, jnp.int32),
            pltpu.SMEM(tags.shape, jnp.int32),
            dma((2, half)), dma((2, half)), dma((2, half)), dma((2, half)),
            dma((half,)), dma((half,)), dma((half,)), dma((half,)),
            dma((2,)), dma((2,)), dma((3,)), dma,
        ],
        compiler_params=pltpu.CompilerParams(
            collective_id=0, has_side_effects=True, vmem_limit_bytes=56 * 1024 * 1024
        ),
        cost_estimate=pl.CostEstimate(
            flops=2 * n * cap * bl * br * (3 * bl + 2 * br),
            bytes_accessed=4 * psi.size + 2 * left.size + 2 * right.size,
            transcendentals=0,
        ),
    )(source, position, tags, psi, left, right)


def shards(psi, block_rows, owner, left_sector, right_sector, left_env, right_env):
    blocks, bl, br = psi.shape
    n = lax.axis_size("sec")
    half = n // 2
    cap = max(2, 2 * blocks // n)
    lsec = left_env.shape[0]
    mine = lax.axis_index("sec") // half
    target = owner[:, 0]
    order = jnp.arange(blocks, dtype=jnp.int32)
    same = target[:, None] == target[None, :]
    earlier = order[None, :] < order[:, None]
    slot = jnp.sum(jnp.where(same & earlier, 1, 0), axis=1).astype(jnp.int32)
    kind = jnp.where(target // half == mine, 0, 1)
    position = (kind * half + target % half) * cap + slot
    slots_all = jnp.arange(n * cap, dtype=jnp.int32)
    match = position[None, :] == slots_all[:, None]
    tag = (right_sector * lsec + left_sector) * (bl + 1) + block_rows
    source = jnp.sum(jnp.where(match, order[None, :], 0), axis=1)
    tags = jnp.sum(jnp.where(match, tag[None, :], 0), axis=1)
    tags = tags.reshape(2, half, cap).transpose(1, 0, 2).reshape(half, 1, 2 * cap)
    tags = jnp.pad(tags, ((0, 0), (0, 0), (0, -(2 * cap) % 128)))
    left = left_env.reshape(lsec, 3 * bl, bl)
    left = jnp.concatenate([left[:, :3 * bl // 2], left[:, 3 * bl // 2:]], axis=2)
    return route(source, position, tags, psi, left, right_env, n, cap, lsec)


def solution(mesh):
    return jax.shard_map(
        shards,
        mesh=mesh,
        in_specs=(
            P(("groups", "sec"), None, None),
            P(("groups", "sec")),
            P(("groups", "sec"), None),
            P(("groups", "sec")),
            P(("groups", "sec")),
            P(("groups", "sec"), None, None, None),
            P(("groups", "sec"), None, None, None),
        ),
        out_specs=P(("groups", "sec"), None, None),
        check_vma=False,
    )
```

```python
import functools

import jax
import jax.numpy as jnp
from jax import lax
from jax.experimental import pallas as pl
from jax.experimental.pallas import tpu as pltpu
from jax.sharding import PartitionSpec as P

F32 = jnp.float32
PLANES = 4
CHUNKS = 8


def route_kernel(
    n, lsec,
    source, position, tags_in, psi, left_in, right_in,
    out,
    sent, got, back, passed, right0, right1, right2, right3, left_p, left_f, tags_v, tags_w, tags_p, tags_f,
    psi_send, psi_recv, ret_send, ret_recv, pass_send, pass_recv, tag_send, tag_recv, tagf_send, tagf_recv,
    left_send, left_recv, leftf_send, leftf_recv, up_send, up_recv, r_send, r_recv, own_sem, self_sem, tag_sem,
):
    plane = n // PLANES
    cap, bl, br = sent.shape[2:]
    rsec = right0.shape[0]
    piece = rsec // CHUNKS
    me = lax.axis_index("sec")
    level = me // plane
    first = level * plane
    mine = me - first
    outer = (level == 0) | (level == PLANES - 1)
    upper = level >= PLANES // 2
    inward = jnp.where(upper, me - plane, me + plane)
    outward = jnp.where(upper, me + plane, me - plane)
    rights = (right0, right1, right2, right3)
    order = (1, 2, 0, 3)

    barrier = pltpu.get_barrier_semaphore()

    def greet(j, c):
        pl.semaphore_signal(barrier, inc=1, device_id={"sec": first + lax.rem(mine + j, plane)})
        return c

    lax.fori_loop(1, plane, greet, 0)
    pl.semaphore_signal(barrier, inc=1, device_id={"sec": inward})

    @pl.when(jnp.logical_not(outer))
    def _():
        pl.semaphore_signal(barrier, inc=1, device_id={"sec": outward})
        pl.semaphore_wait(barrier, plane + 1)

    @pl.when(outer)
    def _():
        pl.semaphore_wait(barrier, plane)

    def remote(src, dst, send, recv, to):
        return pltpu.make_async_remote_copy(
            src_ref=src, dst_ref=dst, send_sem=send, recv_sem=recv, device_id={"sec": to}
        )

    def chunk_copy(src, kind, as_kind, q, to):
        part = pl.ds(q * piece, piece)
        return remote(src.at[part], rights[as_kind].at[part], r_send.at[kind, q], r_recv.at[as_kind, q], to)

    def tag_copy(to, slot):
        return remote(tags_in.at[to], tags_v.at[slot], tag_send.at[to], tag_recv.at[slot], first + to)

    def left_copy(to, slot):
        return remote(left_in, left_p.at[slot], left_send.at[to], left_recv.at[slot], first + to)

    def psi_copy(kind, to, slot):
        return remote(
            sent.at[kind, to], got.at[kind, slot], psi_send.at[kind, to], psi_recv.at[kind, slot], first + to
        )

    def ret_copy(src, kind, to, slot):
        return remote(src, back.at[kind, slot], ret_send.at[kind, to], ret_recv.at[kind, slot], first + to)

    def tagf_copy(s):
        return remote(tags_v.at[s], tags_w.at[s], tagf_send.at[s], tagf_recv.at[s], inward)

    def pass_in(kind, s):
        return remote(
            got.at[kind, s], passed.at[kind - 1, s], pass_send.at[kind - 1, s], pass_recv.at[kind - 1, s], inward
        )

    def pass_back(kind, s):
        return remote(
            passed.at[kind - 1, s], passed.at[kind - 1, s], pass_send.at[kind - 1, s],
            pass_recv.at[kind - 1, s], outward,
        )

    def up_copy():
        return remote(left_in, left_f.at[mine], up_send, up_recv, inward)

    def leftf_copy(to, slot):
        return remote(left_f.at[mine], left_f.at[slot], leftf_send.at[to], leftf_recv.at[slot], first + to)

    def each(work, low=0):
        def one(j, c):
            work(lax.rem(mine + j, plane))
            return c
        lax.fori_loop(low, plane, one, 0)

    def each_from(work, low=0):
        def one(j, c):
            work(lax.rem(mine + plane - j, plane))
            return c
        lax.fori_loop(low, plane, one, 0)

    def start_right(kind, as_kind, to):
        def one(q, c):
            chunk_copy(right_in, kind, as_kind, q, to).start()
            return c
        lax.fori_loop(0, CHUNKS, one, 0)

    def take_right(kind):
        def one(q, c):
            chunk_copy(rights[kind], kind, kind, q, inward).wait_recv()
            return c
        lax.fori_loop(0, CHUNKS, one, 0)

    def end_right(kind, as_kind):
        def one(q, c):
            chunk_copy(right_in, kind, as_kind, q, inward).wait_send()
            return c
        lax.fori_loop(0, CHUNKS, one, 0)

    own_left = pltpu.make_async_copy(left_in, left_p.at[mine], own_sem.at[1])
    own_tags = pltpu.make_async_copy(tags_in.at[mine], tags_v.at[mine], own_sem.at[2])
    own_left.start()
    own_tags.start()

    @pl.when(outer)
    def _():
        start_right(0, 0, inward)
        up_copy().start()

    @pl.when(jnp.logical_not(outer))
    def _():
        start_right(1, 2, inward)

    def send_small(to):
        tag_copy(to, mine).start()
        left_copy(to, mine).start()

    each(send_small, 1)

    def pack(kind, dest, into):
        def one(s, c):
            into[kind, dest, s] = psi[source[(kind * plane + dest) * cap + s]]
            return c
        lax.fori_loop(0, cap, one, 0, unroll=min(cap, 4))

    for kind in order:
        def send_psi(to):
            pack(kind, to, sent)
            psi_copy(kind, to, mine).start()
        each(send_psi, 1)
        pack(kind, mine, got)
    own_tags.wait()
    own_left.wait()

    group = min(cap, 8)
    line = lax.broadcasted_iota(jnp.int32, (bl, br), 0)

    def serve(table, left, blocks, index, kind, src, into, slot):
        def fields(s):
            tag = table[src, 0, kind * cap + s]
            return tag % (bl + 1), (tag // (bl + 1)) % lsec, tag // ((bl + 1) * lsec)

        def one(g, c):
            slots = [g * group + i for i in range(group)]
            parts = []
            for s in slots:
                rows, lsel, _ = fields(s)
                block = jnp.where(line < rows, blocks[index, src, s], jnp.zeros((), jnp.bfloat16))
                packed = left[src, lsel]
                parts.append(jnp.concatenate([
                    jnp.dot(packed[:, :bl], block, preferred_element_type=F32),
                    jnp.dot(packed[:, bl:], block, preferred_element_type=F32),
                ], axis=0))
            for s, made in zip(slots, parts):
                rows, _, rsel = fields(s)
                far = made[:bl]
                for k in range(2):
                    moved = made[(k + 1) * bl:(k + 2) * bl].astype(jnp.bfloat16)
                    far = far + jnp.dot(moved, rights[kind][rsel, k], preferred_element_type=F32)
                into[slot, src, s] = jnp.where(line < rows, far, 0.0).astype(jnp.bfloat16)
            return c

        lax.fori_loop(0, cap // group, one, 0)

    def serve_plane(kind, src):
        @pl.when(src != mine)
        def _():
            psi_copy(kind, src, src).wait_recv()
            serve(tags_p, left_p, got, kind, kind, src, got, kind)
            ret_copy(got.at[kind, src], kind, src, mine).start()

        @pl.when(src == mine)
        def _():
            serve(tags_p, left_p, got, kind, kind, src, back, kind)

    def take_left(src):
        left_copy(src, src).wait_recv()

    def take_tags(src):
        tag_copy(src, src).wait_recv()

    def to_smem(values, table):
        copy = pltpu.make_async_copy(values, table, tag_sem)
        copy.start()
        copy.wait()

    @pl.when(outer)
    def _():
        own = pltpu.make_async_copy(right_in, right0, own_sem.at[0])
        own.start()
        each_from(take_tags, 1)
        each_from(lambda s: tagf_copy(s).start())
        for kind in (1, 2):
            pass_in(kind, mine).start()

            def forward(src):
                psi_copy(kind, src, src).wait_recv()
                pass_in(kind, src).start()
            each_from(forward, 1)
        to_smem(tags_v, tags_p)
        each_from(take_left, 1)
        own.wait()
        each_from(lambda src: serve_plane(0, src))

        def bring(kind, src):
            pass_back(kind, src).wait_recv()

            @pl.when(src != mine)
            def _():
                ret_copy(passed.at[kind - 1, src], kind, src, mine).start()

            @pl.when(src == mine)
            def _():
                pltpu.make_async_copy(passed.at[kind - 1, src], back.at[kind, src], self_sem.at[kind - 1]).start()

        for kind in (1, 2):
            each_from(lambda src: bring(kind, src))
        take_right(3)
        each_from(lambda src: serve_plane(3, src))
        for kind in (1, 2):
            pltpu.make_async_copy(passed.at[kind - 1, mine], back.at[kind, mine], self_sem.at[kind - 1]).wait()

    @pl.when(jnp.logical_not(outer))
    def _():
        own = pltpu.make_async_copy(right_in, right1, own_sem.at[0])
        own.start()
        up_copy().wait_recv()
        each(lambda to: leftf_copy(to, mine).start(), 1)
        each_from(take_tags, 1)
        to_smem(tags_v, tags_p)
        each_from(take_left, 1)
        own.wait()

        def relay_out(q):
            chunk = chunk_copy(right0, 0, 3, q, inward)
            chunk_copy(right0, 0, 0, q, inward).wait_recv()
            chunk.start()

        def relay_back(q):
            chunk_copy(right3, 3, 3, q, outward).wait_recv()
            chunk_copy(right3, 3, 3, q, outward).start()

        def serve_passed(kind, src):
            pass_in(kind, src).wait_recv()
            serve(tags_f, left_f, passed, kind - 1, kind, src, passed, kind - 1)
            pass_back(kind, src).start()

        steps = CHUNKS // 2
        share = plane // steps

        def early(work):
            def some(q):
                def one(i, c):
                    work(lax.rem(mine + plane - (q * share + i), plane))
                    return c
                lax.fori_loop(0, share, one, 0)
            return some

        def phase(low, work):
            def one(q, c):
                relay_out(q + low)

                @pl.when(q + low > 0)
                def _():
                    relay_back(q + low - 1)
                work(q)
                return c
            lax.fori_loop(0, steps, one, 0)

        phase(0, early(lambda src: serve_plane(1, src)))
        each_from(lambda s: tagf_copy(s).wait_recv())
        to_smem(tags_w, tags_f)
        each_from(lambda src: leftf_copy(src, src).wait_recv(), 1)
        phase(steps, early(lambda src: serve_passed(1, src)))
        relay_back(CHUNKS - 1)
        take_right(2)
        each_from(lambda src: serve_passed(2, src))
        each_from(lambda src: serve_plane(2, src))
        each_from(lambda src: serve_plane(0, src))
        each_from(lambda src: serve_plane(3, src))

    for kind in order:
        each_from(lambda src: ret_copy(back.at[kind, src], kind, src, src).wait_recv(), 1)

    def unpack(i, c):
        p = position[i]
        out[i] = back[p // (plane * cap), (p // cap) % plane, p % cap]
        return c

    lax.fori_loop(0, out.shape[0], unpack, 0, unroll=4)

    def finish(to):
        tag_copy(to, mine).wait_send()
        left_copy(to, mine).wait_send()
        for kind in range(4):
            psi_copy(kind, to, mine).wait_send()
            ret_copy(got.at[kind, to], kind, to, mine).wait_send()

    each(finish, 1)

    @pl.when(outer)
    def _():
        end_right(0, 0)
        up_copy().wait_send()
        each(lambda s: tagf_copy(s).wait_send())
        for kind in (1, 2):
            each(lambda s: pass_in(kind, s).wait_send())

    @pl.when(jnp.logical_not(outer))
    def _():
        end_right(1, 2)
        end_right(0, 3)
        end_right(3, 3)
        each(lambda to: leftf_copy(to, mine).wait_send(), 1)
        for kind in (1, 2):
            each(lambda s: pass_back(kind, s).wait_send())


def route(source, position, tags, psi, left, right, n, cap, lsec):
    plane = n // PLANES
    blocks, bl, br = psi.shape
    slots = (4, plane, cap, bl, br)
    vmem, smem = pl.BlockSpec(memory_space=pltpu.VMEM), pl.BlockSpec(memory_space=pltpu.SMEM)
    dma = pltpu.SemaphoreType.DMA
    return pl.pallas_call(
        functools.partial(route_kernel, n, lsec),
        out_shape=jax.ShapeDtypeStruct(psi.shape, jnp.bfloat16),
        in_specs=[smem, smem, vmem, vmem, vmem, pl.BlockSpec(memory_space=pl.ANY)],
        out_specs=vmem,
        scratch_shapes=[
            pltpu.VMEM(slots, jnp.bfloat16),
            pltpu.VMEM(slots, jnp.bfloat16),
            pltpu.VMEM(slots, jnp.bfloat16),
            pltpu.VMEM((2,) + slots[1:], jnp.bfloat16),
            pltpu.VMEM(right.shape, jnp.bfloat16),
            pltpu.VMEM(right.shape, jnp.bfloat16),
            pltpu.VMEM(right.shape, jnp.bfloat16),
            pltpu.VMEM(right.shape, jnp.bfloat16),
            pltpu.VMEM((plane,) + left.shape, jnp.bfloat16),
            pltpu.VMEM((plane,) + left.shape, jnp.bfloat16),
            pltpu.VMEM(tags.shape, jnp.int32),
            pltpu.VMEM(tags.shape, jnp.int32),
            pltpu.SMEM(tags.shape, jnp.int32),
            pltpu.SMEM(tags.shape, jnp.int32),
            dma((4, plane)), dma((4, plane)), dma((4, plane)), dma((4, plane)),
            dma((2, plane)), dma((2, plane)),
            dma((plane,)), dma((plane,)), dma((plane,)), dma((plane,)),
            dma((plane,)), dma((plane,)), dma((plane,)), dma((plane,)),
            dma, dma, dma((4, CHUNKS)), dma((4, CHUNKS)), dma((3,)), dma((2,)), dma,
        ],
        compiler_params=pltpu.CompilerParams(
            collective_id=0, has_side_effects=True, vmem_limit_bytes=56 * 1024 * 1024
        ),
        cost_estimate=pl.CostEstimate(
            flops=2 * n * cap * bl * br * (3 * bl + 2 * br),
            bytes_accessed=4 * psi.size + 2 * left.size + 2 * right.size,
            transcendentals=0,
        ),
    )(source, position, tags, psi, left, right)


def shards(psi, block_rows, owner, left_sector, right_sector, left_env, right_env):
    blocks, bl, br = psi.shape
    n = lax.axis_size("sec")
    plane = n // PLANES
    cap = max(2, 2 * blocks // n)
    lsec = left_env.shape[0]
    upper = lax.axis_index("sec") // plane >= PLANES // 2
    target = owner[:, 0]
    order = jnp.arange(blocks, dtype=jnp.int32)
    same = target[:, None] == target[None, :]
    earlier = order[None, :] < order[:, None]
    slot = jnp.sum(jnp.where(same & earlier, 1, 0), axis=1).astype(jnp.int32)
    level = target // plane
    kind = jnp.where(upper, PLANES - 1 - level, level)
    position = (kind * plane + target % plane) * cap + slot
    slots_all = jnp.arange(n * cap, dtype=jnp.int32)
    match = position[None, :] == slots_all[:, None]
    tag = (right_sector * lsec + left_sector) * (bl + 1) + block_rows
    source = jnp.sum(jnp.where(match, order[None, :], 0), axis=1)
    tags = jnp.sum(jnp.where(match, tag[None, :], 0), axis=1)
    tags = tags.reshape(4, plane, cap).transpose(1, 0, 2).reshape(plane, 1, 4 * cap)
    tags = jnp.pad(tags, ((0, 0), (0, 0), (0, -(4 * cap) % 128)))
    left = left_env.reshape(lsec, 3 * bl, bl)
    left = jnp.concatenate([left[:, :3 * bl // 2], left[:, 3 * bl // 2:]], axis=2)
    return route(source, position, tags, psi, left, right_env, n, cap, lsec)


def solution(mesh):
    return jax.shard_map(
        shards,
        mesh=mesh,
        in_specs=(
            P(("groups", "sec"), None, None),
            P(("groups", "sec")),
            P(("groups", "sec"), None),
            P(("groups", "sec")),
            P(("groups", "sec")),
            P(("groups", "sec"), None, None, None),
            P(("groups", "sec"), None, None, None),
        ),
        out_specs=P(("groups", "sec"), None, None),
        check_vma=False,
    )
```

```python
import functools

import jax
import jax.numpy as jnp
from jax import lax
from jax.experimental import pallas as pl
from jax.experimental.pallas import tpu as pltpu
from jax.sharding import PartitionSpec as P

F32 = jnp.float32


def route_kernel(
    n, lsec,
    source, position, tags_in, psi, left_in, right_in,
    out,
    sent, got, back, total, right, mirror0, mirror1, left, tags_v, tags,
    psi_send, psi_recv, ret_send, ret_recv, tag_send, tag_recv, left_send, left_recv,
    mir_send, mir_recv, own_sem, tag_sem,
):
    half = n // 2
    cap, bl, br = sent.shape[2:]
    me = lax.axis_index("sec")
    first = (me // half) * half
    mine = me - first
    partner = lax.rem(me + half, n)
    quarter = half // 2
    corner = (mine // quarter) * quarter
    across = lax.rem(mine + quarter, half)

    barrier = pltpu.get_barrier_semaphore()

    def greet(j, c):
        pl.semaphore_signal(barrier, inc=1, device_id={"sec": first + lax.rem(mine + j, half)})
        return c

    lax.fori_loop(1, half, greet, 0)
    pl.semaphore_signal(barrier, inc=1, device_id={"sec": partner})
    pl.semaphore_wait(barrier, half)

    mirrors = (mirror0, mirror1)

    def mirror_copy(k):
        return pltpu.make_async_remote_copy(
            src_ref=right_in.at[:, k], dst_ref=mirrors[k], send_sem=mir_send.at[k],
            recv_sem=mir_recv.at[k], device_id={"sec": partner},
        )

    def tag_copy(to, slot):
        return pltpu.make_async_remote_copy(
            src_ref=tags_in.at[to], dst_ref=tags_v.at[slot], send_sem=tag_send.at[to],
            recv_sem=tag_recv.at[slot], device_id={"sec": first + to},
        )

    def left_copy(src, to, slot, sem):
        return pltpu.make_async_remote_copy(
            src_ref=src, dst_ref=left.at[slot], send_sem=left_send.at[sem, to],
            recv_sem=left_recv.at[slot], device_id={"sec": first + to},
        )

    def beside(j):
        return corner + lax.rem(mine - corner + j, quarter)

    def psi_copy(kind, to, slot):
        return pltpu.make_async_remote_copy(
            src_ref=sent.at[kind, to], dst_ref=got.at[kind, slot], send_sem=psi_send.at[kind, to],
            recv_sem=psi_recv.at[kind, slot], device_id={"sec": first + to},
        )

    def ret_copy(kind, to, slot):
        return pltpu.make_async_remote_copy(
            src_ref=got.at[kind, to], dst_ref=back.at[kind, slot], send_sem=ret_send.at[kind, to],
            recv_sem=ret_recv.at[kind, slot], device_id={"sec": first + to},
        )

    mirror_copy(0).start()
    mirror_copy(1).start()
    own = [
        pltpu.make_async_copy(right_in, right, own_sem.at[0]),
        pltpu.make_async_copy(left_in, left.at[mine], own_sem.at[1]),
        pltpu.make_async_copy(tags_in.at[mine], tags_v.at[mine], own_sem.at[2]),
    ]
    for copy in own:
        copy.start()

    def send_small(j, c):
        to = lax.rem(mine + j, half)
        tag_copy(to, mine).start()
        return c

    def send_left(j, c):
        left_copy(left_in, beside(j), mine, 0).start()
        return c

    def hand_left(j, c):
        left_copy(left.at[across], beside(j), across, 1).start()
        return c

    left_copy(left_in, across, mine, 0).start()
    lax.fori_loop(1, half, send_small, 0)
    lax.fori_loop(1, quarter, send_left, 0)

    def pack(kind, dest, into):
        def one(s, c):
            into[kind, dest, s] = psi[source[(kind * half + dest) * cap + s]]
            return c
        lax.fori_loop(0, cap, one, 0, unroll=min(cap, 4))

    for kind in range(2):
        def send_psi(j, c):
            to = lax.rem(mine + j, half)
            pack(kind, to, sent)
            psi_copy(kind, to, mine).start()
            return c
        lax.fori_loop(1, half, send_psi, 0)
        pack(kind, mine, got)

    left_copy(left_in, across, across, 0).wait_recv()
    lax.fori_loop(1, quarter, hand_left, 0)

    for copy in own:
        copy.wait()

    def take_small(j, c):
        src = lax.rem(mine + half - j, half)
        tag_copy(src, src).wait_recv()
        return c

    def take_left(j, c):
        src = beside(j)
        left_copy(left_in, src, src, 0).wait_recv()
        src = lax.rem(src + quarter, half)
        left_copy(left_in, src, src, 0).wait_recv()
        return c

    lax.fori_loop(1, half, take_small, 0)
    lax.fori_loop(1, quarter, take_left, 0)
    copy = pltpu.make_async_copy(tags_v, tags, tag_sem)
    copy.start()
    copy.wait()

    group = min(cap, 8)
    line = lax.broadcasted_iota(jnp.int32, (bl, br), 0)

    def fields(kind, src, s):
        tag = tags[src, 0, kind * cap + s]
        return tag % (bl + 1), (tag // (bl + 1)) % lsec, tag // ((bl + 1) * lsec)

    def contract_left(kind, src, s):
        rows, lsel, _ = fields(kind, src, s)
        block = jnp.where(line < rows, got[kind, src, s], jnp.zeros((), jnp.bfloat16))
        packed = left[src, lsel]
        made = jnp.concatenate([
            jnp.dot(packed[:, :bl], block, preferred_element_type=F32),
            jnp.dot(packed[:, bl:], block, preferred_element_type=F32),
        ], axis=0)
        return made[:bl], made[bl:2 * bl].astype(jnp.bfloat16), made[2 * bl:].astype(jnp.bfloat16)

    def over_groups(work):
        def one(g, c):
            work([g * group + i for i in range(group)])
            return c
        lax.fori_loop(0, cap // group, one, 0)

    def whole(kind, src, into):
        def work(slots):
            parts = [contract_left(kind, src, s) for s in slots]
            for s, (local, m0, m1) in zip(slots, parts):
                rows, _, rsel = fields(kind, src, s)
                far = jnp.dot(m0, right[rsel, 0], preferred_element_type=F32)
                far = far + jnp.dot(m1, right[rsel, 1], preferred_element_type=F32)
                into[kind, src, s] = jnp.where(line < rows, local + far, 0.0).astype(jnp.bfloat16)
        over_groups(work)

    def first_term(src):
        def work(slots):
            parts = [contract_left(1, src, s) for s in slots]
            for s, (local, m0, m1) in zip(slots, parts):
                _, _, rsel = fields(1, src, s)
                total[src, s] = local + jnp.dot(m0, mirror0[rsel], preferred_element_type=F32)
                got[1, src, s] = m1
        over_groups(work)

    def second_term(src, into):
        def work(slots):
            for s in slots:
                rows, _, rsel = fields(1, src, s)
                far = total[src, s] + jnp.dot(got[1, src, s], mirror1[rsel], preferred_element_type=F32)
                into[1, src, s] = jnp.where(line < rows, far, 0.0).astype(jnp.bfloat16)
        over_groups(work)

    def serve_near(j, c):
        src = lax.rem(mine + half - j, half)
        psi_copy(0, src, src).wait_recv()
        whole(0, src, got)
        ret_copy(0, src, mine).start()
        return c

    lax.fori_loop(1, half, serve_near, 0)
    whole(0, mine, back)

    mirror_copy(0).wait_recv()

    def begin_far(j, c):
        src = lax.rem(mine + half - j, half)
        psi_copy(1, src, src).wait_recv()
        first_term(src)
        return c

    lax.fori_loop(1, half, begin_far, 0)
    first_term(mine)

    mirror_copy(1).wait_recv()

    def end_far(j, c):
        src = lax.rem(mine + half - j, half)
        second_term(src, got)
        ret_copy(1, src, mine).start()
        return c

    lax.fori_loop(1, half, end_far, 0)
    second_term(mine, back)

    def take_back(j, c):
        src = lax.rem(mine + half - j, half)
        ret_copy(0, src, src).wait_recv()
        ret_copy(1, src, src).wait_recv()
        return c

    lax.fori_loop(1, half, take_back, 0)

    def unpack(i, c):
        p = position[i]
        out[i] = back[p // (half * cap), (p // cap) % half, p % cap]
        return c

    lax.fori_loop(0, out.shape[0], unpack, 0, unroll=4)

    def finish(j, c):
        to = lax.rem(mine + j, half)
        tag_copy(to, mine).wait_send()
        for kind in range(2):
            psi_copy(kind, to, mine).wait_send()
            ret_copy(kind, to, mine).wait_send()
        return c

    def finish_left(j, c):
        left_copy(left_in, beside(j), mine, 0).wait_send()
        left_copy(left_in, beside(j), across, 1).wait_send()
        return c

    lax.fori_loop(1, half, finish, 0)
    lax.fori_loop(1, quarter, finish_left, 0)
    left_copy(left_in, across, mine, 0).wait_send()
    for k in range(2):
        mirror_copy(k).wait_send()


def route(source, position, tags, psi, left, right, n, cap, lsec):
    half = n // 2
    blocks, bl, br = psi.shape
    rsec = right.shape[0]
    slots = (2, half, cap, bl, br)
    vmem, smem = pl.BlockSpec(memory_space=pltpu.VMEM), pl.BlockSpec(memory_space=pltpu.SMEM)
    dma = pltpu.SemaphoreType.DMA
    return pl.pallas_call(
        functools.partial(route_kernel, n, lsec),
        out_shape=jax.ShapeDtypeStruct(psi.shape, jnp.bfloat16),
        in_specs=[smem, smem, vmem, vmem, vmem, pl.BlockSpec(memory_space=pl.ANY)],
        out_specs=vmem,
        scratch_shapes=[
            pltpu.VMEM(slots, jnp.bfloat16),
            pltpu.VMEM(slots, jnp.bfloat16),
            pltpu.VMEM(slots, jnp.bfloat16),
            pltpu.VMEM(slots[1:], F32),
            pltpu.VMEM(right.shape, jnp.bfloat16),
            pltpu.VMEM((rsec, br, br), jnp.bfloat16),
            pltpu.VMEM((rsec, br, br), jnp.bfloat16),
            pltpu.VMEM((half,) + left.shape, jnp.bfloat16),
            pltpu.VMEM(tags.shape, jnp.int32),
            pltpu.SMEM(tags.shape, jnp.int32),
            dma((2, half)), dma((2, half)), dma((2, half)), dma((2, half)),
            dma((half,)), dma((half,)), dma((2, half)), dma((half,)),
            dma((2,)), dma((2,)), dma((3,)), dma,
        ],
        compiler_params=pltpu.CompilerParams(
            collective_id=0, has_side_effects=True, vmem_limit_bytes=56 * 1024 * 1024
        ),
        cost_estimate=pl.CostEstimate(
            flops=2 * n * cap * bl * br * (3 * bl + 2 * br),
            bytes_accessed=4 * psi.size + 2 * left.size + 2 * right.size,
            transcendentals=0,
        ),
    )(source, position, tags, psi, left, right)


def shards(psi, block_rows, owner, left_sector, right_sector, left_env, right_env):
    blocks, bl, br = psi.shape
    n = lax.axis_size("sec")
    half = n // 2
    cap = max(2, 2 * blocks // n)
    lsec = left_env.shape[0]
    mine = lax.axis_index("sec") // half
    target = owner[:, 0]
    order = jnp.arange(blocks, dtype=jnp.int32)
    same = target[:, None] == target[None, :]
    earlier = order[None, :] < order[:, None]
    slot = jnp.sum(jnp.where(same & earlier, 1, 0), axis=1).astype(jnp.int32)
    kind = jnp.where(target // half == mine, 0, 1)
    position = (kind * half + target % half) * cap + slot
    slots_all = jnp.arange(n * cap, dtype=jnp.int32)
    match = position[None, :] == slots_all[:, None]
    tag = (right_sector * lsec + left_sector) * (bl + 1) + block_rows
    source = jnp.sum(jnp.where(match, order[None, :], 0), axis=1)
    tags = jnp.sum(jnp.where(match, tag[None, :], 0), axis=1)
    tags = tags.reshape(2, half, cap).transpose(1, 0, 2).reshape(half, 1, 2 * cap)
    tags = jnp.pad(tags, ((0, 0), (0, 0), (0, -(2 * cap) % 128)))
    left = left_env.reshape(lsec, 3 * bl, bl)
    left = jnp.concatenate([left[:, :3 * bl // 2], left[:, 3 * bl // 2:]], axis=2)
    return route(source, position, tags, psi, left, right_env, n, cap, lsec)


def solution(mesh):
    return jax.shard_map(
        shards,
        mesh=mesh,
        in_specs=(
            P(("groups", "sec"), None, None),
            P(("groups", "sec")),
            P(("groups", "sec"), None),
            P(("groups", "sec")),
            P(("groups", "sec")),
            P(("groups", "sec"), None, None, None),
            P(("groups", "sec"), None, None, None),
        ),
        out_specs=P(("groups", "sec"), None, None),
        check_vma=False,
    )
```

```python
import functools

import jax
import jax.numpy as jnp
from jax import lax
from jax.experimental import pallas as pl
from jax.experimental.pallas import tpu as pltpu
from jax.sharding import PartitionSpec as P

F32 = jnp.float32
PIECES = 4


def route_kernel(
    n, lsec,
    source, position, tags_in, psi, left_in, right_in,
    out,
    sent, got, back, total, right, mirror0, mirror1, near0, near1, left, tags_v, tags,
    psi_send, psi_recv, ret_send, ret_recv, tag_send, tag_recv, left_send, left_recv,
    mir_send, mir_recv, hop_send, hop_recv, own_sem, tag_sem,
):
    half = n // 2
    cap, bl, br = sent.shape[2:]
    me = lax.axis_index("sec")
    first = (me // half) * half
    mine = me - first
    partner = lax.rem(me + half, n)
    quarter = half // 2
    corner = (mine // quarter) * quarter
    across = lax.rem(mine + quarter, half)
    outer = (first == 0) == (corner == 0)
    facing = lax.rem(first + across + half, n)
    piece = right_in.shape[0] // PIECES

    barrier = pltpu.get_barrier_semaphore()

    def greet(j, c):
        pl.semaphore_signal(barrier, inc=1, device_id={"sec": first + lax.rem(mine + j, half)})
        return c

    lax.fori_loop(1, half, greet, 0)
    pl.semaphore_signal(barrier, inc=1, device_id={"sec": partner})

    @pl.when(outer)
    def _():
        pl.semaphore_wait(barrier, half)

    @pl.when(jnp.logical_not(outer))
    def _():
        pl.semaphore_signal(barrier, inc=1, device_id={"sec": facing})
        pl.semaphore_wait(barrier, half + 1)

    mirrors, nears = (mirror0, mirror1), (near0, near1)

    def mirror_copy(k, q):
        part = pl.ds(q * piece, piece)
        return pltpu.make_async_remote_copy(
            src_ref=right_in.at[part, k], dst_ref=mirrors[k].at[part], send_sem=mir_send.at[k, q],
            recv_sem=mir_recv.at[k, q], device_id={"sec": partner},
        )

    def hop_copy(k, q):
        part = pl.ds(q * piece, piece)
        return pltpu.make_async_remote_copy(
            src_ref=right_in.at[part, k], dst_ref=nears[k].at[part], send_sem=hop_send.at[k, q],
            recv_sem=hop_recv.at[k, q], device_id={"sec": first + across},
        )

    def relay_copy(k, q):
        part = pl.ds(q * piece, piece)
        return pltpu.make_async_remote_copy(
            src_ref=nears[k].at[part], dst_ref=mirrors[k].at[part], send_sem=hop_send.at[k, q],
            recv_sem=mir_recv.at[k, q], device_id={"sec": facing},
        )

    def pieces(work):
        for k in range(2):
            def one(q, c):
                work(k, q)
                return c
            lax.fori_loop(0, PIECES, one, 0)

    def tag_copy(to, slot):
        return pltpu.make_async_remote_copy(
            src_ref=tags_in.at[to], dst_ref=tags_v.at[slot], send_sem=tag_send.at[to],
            recv_sem=tag_recv.at[slot], device_id={"sec": first + to},
        )

    def left_copy(src, to, slot, sem):
        return pltpu.make_async_remote_copy(
            src_ref=src, dst_ref=left.at[slot], send_sem=left_send.at[sem, to],
            recv_sem=left_recv.at[slot], device_id={"sec": first + to},
        )

    def beside(j):
        return corner + lax.rem(mine - corner + j, quarter)

    def psi_copy(kind, to, slot):
        return pltpu.make_async_remote_copy(
            src_ref=sent.at[kind, to], dst_ref=got.at[kind, slot], send_sem=psi_send.at[kind, to],
            recv_sem=psi_recv.at[kind, slot], device_id={"sec": first + to},
        )

    def aside_copy(to, at, slot):
        return pltpu.make_async_remote_copy(
            src_ref=sent.at[0, to], dst_ref=got.at[2, slot], send_sem=psi_send.at[0, to],
            recv_sem=psi_recv.at[2, slot], device_id={"sec": first + at},
        )

    def aside_ret(to, slot):
        return pltpu.make_async_remote_copy(
            src_ref=got.at[2, to], dst_ref=back.at[0, slot], send_sem=ret_send.at[2, to],
            recv_sem=ret_recv.at[0, slot], device_id={"sec": first + to},
        )

    def ret_copy(kind, to, slot):
        return pltpu.make_async_remote_copy(
            src_ref=got.at[kind, to], dst_ref=back.at[kind, slot], send_sem=ret_send.at[kind, to],
            recv_sem=ret_recv.at[kind, slot], device_id={"sec": first + to},
        )

    @pl.when(outer)
    def _():
        pieces(lambda k, q: hop_copy(k, q).start())

    @pl.when(jnp.logical_not(outer))
    def _():
        pieces(lambda k, q: mirror_copy(k, q).start())

    own = [
        pltpu.make_async_copy(right_in, right, own_sem.at[0]),
        pltpu.make_async_copy(left_in, left.at[mine], own_sem.at[1]),
        pltpu.make_async_copy(tags_in.at[mine], tags_v.at[mine], own_sem.at[2]),
    ]
    for copy in own:
        copy.start()

    def send_small(j, c):
        to = lax.rem(mine + j, half)
        tag_copy(to, mine).start()
        return c

    def send_left(j, c):
        left_copy(left_in, beside(j), mine, 0).start()
        return c

    def hand_left(j, c):
        left_copy(left.at[across], beside(j), across, 1).start()
        return c

    left_copy(left_in, across, mine, 0).start()
    lax.fori_loop(1, half, send_small, 0)
    lax.fori_loop(1, quarter, send_left, 0)

    def pack(kind, dest, into, at_kind=None, at=None):
        at_kind, at = (kind, dest) if at is None else (at_kind, at)

        def one(s, c):
            into[at_kind, at, s] = psi[source[(kind * half + dest) * cap + s]]
            return c
        lax.fori_loop(0, cap, one, 0, unroll=min(cap, 4))

    for kind in range(2):
        def send_psi(j, c):
            to = lax.rem(mine + j, half)
            aside = jnp.logical_not(outer) & (to // quarter != mine // quarter) & (kind == 0)
            at = lax.rem(to + quarter, half)

            @pl.when(jnp.logical_not(aside))
            def _():
                pack(kind, to, sent)
                psi_copy(kind, to, mine).start()

            if kind == 0:
                @pl.when(aside & (at != mine))
                def _():
                    pack(0, to, sent)
                    aside_copy(to, at, mine).start()

                @pl.when(aside & (at == mine))
                def _():
                    pack(0, to, got, 2, mine)
            return c
        lax.fori_loop(1, half, send_psi, 0)
        pack(kind, mine, got)

    left_copy(left_in, across, across, 0).wait_recv()
    lax.fori_loop(1, quarter, hand_left, 0)

    for copy in own:
        copy.wait()

    def take_small(j, c):
        src = lax.rem(mine + half - j, half)
        tag_copy(src, src).wait_recv()
        return c

    def take_left(j, c):
        src = beside(j)
        left_copy(left_in, src, src, 0).wait_recv()
        src = lax.rem(src + quarter, half)
        left_copy(left_in, src, src, 0).wait_recv()
        return c

    lax.fori_loop(1, half, take_small, 0)
    lax.fori_loop(1, quarter, take_left, 0)
    copy = pltpu.make_async_copy(tags_v, tags, tag_sem)
    copy.start()
    copy.wait()

    group = min(cap, 8)
    line = lax.broadcasted_iota(jnp.int32, (bl, br), 0)

    def fields(kind, src, s):
        tag = tags[src, 0, kind * cap + s]
        return tag % (bl + 1), (tag // (bl + 1)) % lsec, tag // ((bl + 1) * lsec)

    def contract_left(kind, src, s):
        rows, lsel, _ = fields(kind, src, s)
        block = jnp.where(line < rows, got[kind, src, s], jnp.zeros((), jnp.bfloat16))
        packed = left[src, lsel]
        made = jnp.concatenate([
            jnp.dot(packed[:, :bl], block, preferred_element_type=F32),
            jnp.dot(packed[:, bl:], block, preferred_element_type=F32),
        ], axis=0)
        return made[:bl], made[bl:2 * bl].astype(jnp.bfloat16), made[2 * bl:].astype(jnp.bfloat16)

    def over_groups(work):
        def one(g, c):
            work([g * group + i for i in range(group)])
            return c
        lax.fori_loop(0, cap // group, one, 0)

    def whole(kind, src, into, at_kind, at):
        def work(slots):
            parts = [contract_left(kind, src, s) for s in slots]
            for s, (local, m0, m1) in zip(slots, parts):
                rows, _, rsel = fields(kind, src, s)
                r0, r1 = (near0[rsel], near1[rsel]) if kind == 2 else (right[rsel, 0], right[rsel, 1])
                far = jnp.dot(m0, r0, preferred_element_type=F32)
                far = far + jnp.dot(m1, r1, preferred_element_type=F32)
                into[at_kind, at, s] = jnp.where(line < rows, local + far, 0.0).astype(jnp.bfloat16)
        over_groups(work)

    def first_term(src):
        def work(slots):
            parts = [contract_left(1, src, s) for s in slots]
            for s, (local, m0, m1) in zip(slots, parts):
                _, _, rsel = fields(1, src, s)
                total[src, s] = local + jnp.dot(m0, mirror0[rsel], preferred_element_type=F32)
                got[1, src, s] = m1
        over_groups(work)

    def second_term(src, into):
        def work(slots):
            for s in slots:
                rows, _, rsel = fields(1, src, s)
                far = total[src, s] + jnp.dot(got[1, src, s], mirror1[rsel], preferred_element_type=F32)
                into[1, src, s] = jnp.where(line < rows, far, 0.0).astype(jnp.bfloat16)
        over_groups(work)

    def serve_near(src):
        psi_copy(0, src, src).wait_recv()
        whole(0, src, got, 0, src)
        ret_copy(0, src, mine).start()

    def serve_beside(j, c):
        serve_near(beside(j))
        return c

    def serve_aside(j, c):
        src = beside(j)
        aside_copy(src, src, src).wait_recv()
        whole(2, src, got, 2, src)
        aside_ret(src, across).start()
        return c

    @pl.when(outer)
    def _():
        lax.fori_loop(1, quarter, serve_beside, 0)
        whole(0, mine, back, 0, mine)

    @pl.when(jnp.logical_not(outer))
    def _():
        share = quarter // PIECES

        def relay_and_serve(k):
            def one(q, c):
                hop_copy(k, q).wait_recv()
                relay_copy(k, q).start()

                def some(i, c):
                    j = q * share + i
                    if k == 0:
                        @pl.when(j > 0)
                        def _():
                            serve_near(beside(j))

                        @pl.when(j == 0)
                        def _():
                            whole(0, mine, back, 0, mine)
                    else:
                        serve_near(lax.rem(beside(j) + quarter, half))
                    return c
                lax.fori_loop(0, share, some, 0)
                return c
            lax.fori_loop(0, PIECES, one, 0)

        relay_and_serve(0)
        relay_and_serve(1)
        lax.fori_loop(1, quarter, serve_aside, 0)
        whole(2, mine, back, 0, across)

    def take_mirror(k):
        def one(q, c):
            mirror_copy(k, q).wait_recv()
            return c
        lax.fori_loop(0, PIECES, one, 0)

    take_mirror(0)

    def begin_far(j, c):
        src = lax.rem(mine + half - j, half)
        psi_copy(1, src, src).wait_recv()
        first_term(src)
        return c

    lax.fori_loop(1, half, begin_far, 0)
    first_term(mine)

    take_mirror(1)

    def end_far(j, c):
        src = lax.rem(mine + half - j, half)
        second_term(src, got)
        ret_copy(1, src, mine).start()
        return c

    lax.fori_loop(1, half, end_far, 0)
    second_term(mine, back)

    def take_back(j, c):
        src = lax.rem(mine + half - j, half)

        @pl.when(outer | (src != across))
        def _():
            ret_copy(0, src, src).wait_recv()
        ret_copy(1, src, src).wait_recv()
        return c

    lax.fori_loop(1, half, take_back, 0)

    def unpack(i, c):
        p = position[i]
        out[i] = back[p // (half * cap), (p // cap) % half, p % cap]
        return c

    lax.fori_loop(0, out.shape[0], unpack, 0, unroll=4)

    def finish(j, c):
        to = lax.rem(mine + j, half)
        tag_copy(to, mine).wait_send()
        near = to // quarter == mine // quarter

        @pl.when(outer | (to != across))
        def _():
            psi_copy(0, to, mine).wait_send()

        @pl.when(jnp.logical_not(outer) | near)
        def _():
            ret_copy(0, to, mine).wait_send()

        @pl.when(jnp.logical_not(outer) & near)
        def _():
            aside_ret(to, across).wait_send()
        psi_copy(1, to, mine).wait_send()
        ret_copy(1, to, mine).wait_send()
        return c

    def finish_left(j, c):
        left_copy(left_in, beside(j), mine, 0).wait_send()
        left_copy(left_in, beside(j), across, 1).wait_send()
        return c

    lax.fori_loop(1, half, finish, 0)
    lax.fori_loop(1, quarter, finish_left, 0)
    left_copy(left_in, across, mine, 0).wait_send()
    pieces(lambda k, q: hop_copy(k, q).wait_send())

    @pl.when(jnp.logical_not(outer))
    def _():
        pieces(lambda k, q: mirror_copy(k, q).wait_send())


def route(source, position, tags, psi, left, right, n, cap, lsec):
    half = n // 2
    blocks, bl, br = psi.shape
    rsec = right.shape[0]
    slots = (2, half, cap, bl, br)
    vmem, smem = pl.BlockSpec(memory_space=pltpu.VMEM), pl.BlockSpec(memory_space=pltpu.SMEM)
    dma = pltpu.SemaphoreType.DMA
    return pl.pallas_call(
        functools.partial(route_kernel, n, lsec),
        out_shape=jax.ShapeDtypeStruct(psi.shape, jnp.bfloat16),
        in_specs=[smem, smem, vmem, vmem, vmem, pl.BlockSpec(memory_space=pl.ANY)],
        out_specs=vmem,
        scratch_shapes=[
            pltpu.VMEM(slots, jnp.bfloat16),
            pltpu.VMEM((3,) + slots[1:], jnp.bfloat16),
            pltpu.VMEM(slots, jnp.bfloat16),
            pltpu.VMEM(slots[1:], F32),
            pltpu.VMEM(right.shape, jnp.bfloat16),
            pltpu.VMEM((rsec, br, br), jnp.bfloat16),
            pltpu.VMEM((rsec, br, br), jnp.bfloat16),
            pltpu.VMEM((rsec, br, br), jnp.bfloat16),
            pltpu.VMEM((rsec, br, br), jnp.bfloat16),
            pltpu.VMEM((half,) + left.shape, jnp.bfloat16),
            pltpu.VMEM(tags.shape, jnp.int32),
            pltpu.SMEM(tags.shape, jnp.int32),
            dma((2, half)), dma((3, half)), dma((3, half)), dma((2, half)),
            dma((half,)), dma((half,)), dma((2, half)), dma((half,)),
            dma((2, PIECES)), dma((2, PIECES)), dma((2, PIECES)), dma((2, PIECES)), dma((3,)), dma,
        ],
        compiler_params=pltpu.CompilerParams(
            collective_id=0, has_side_effects=True, vmem_limit_bytes=56 * 1024 * 1024
        ),
        cost_estimate=pl.CostEstimate(
            flops=2 * n * cap * bl * br * (3 * bl + 2 * br),
            bytes_accessed=4 * psi.size + 2 * left.size + 2 * right.size,
            transcendentals=0,
        ),
    )(source, position, tags, psi, left, right)


def shards(psi, block_rows, owner, left_sector, right_sector, left_env, right_env):
    blocks, bl, br = psi.shape
    n = lax.axis_size("sec")
    half = n // 2
    cap = max(2, 2 * blocks // n)
    lsec = left_env.shape[0]
    mine = lax.axis_index("sec") // half
    target = owner[:, 0]
    order = jnp.arange(blocks, dtype=jnp.int32)
    same = target[:, None] == target[None, :]
    earlier = order[None, :] < order[:, None]
    slot = jnp.sum(jnp.where(same & earlier, 1, 0), axis=1).astype(jnp.int32)
    kind = jnp.where(target // half == mine, 0, 1)
    position = (kind * half + target % half) * cap + slot
    slots_all = jnp.arange(n * cap, dtype=jnp.int32)
    match = position[None, :] == slots_all[:, None]
    tag = (right_sector * lsec + left_sector) * (bl + 1) + block_rows
    source = jnp.sum(jnp.where(match, order[None, :], 0), axis=1)
    tags = jnp.sum(jnp.where(match, tag[None, :], 0), axis=1)
    tags = tags.reshape(2, half, cap)
    tags = jnp.concatenate([tags, jnp.roll(tags[:1], half // 2, axis=1)], axis=0)
    tags = tags.transpose(1, 0, 2).reshape(half, 1, 3 * cap)
    tags = jnp.pad(tags, ((0, 0), (0, 0), (0, -(3 * cap) % 128)))
    left = left_env.reshape(lsec, 3 * bl, bl)
    left = jnp.concatenate([left[:, :3 * bl // 2], left[:, 3 * bl // 2:]], axis=2)
    return route(source, position, tags, psi, left, right_env, n, cap, lsec)


def solution(mesh):
    return jax.shard_map(
        shards,
        mesh=mesh,
        in_specs=(
            P(("groups", "sec"), None, None),
            P(("groups", "sec")),
            P(("groups", "sec"), None),
            P(("groups", "sec")),
            P(("groups", "sec")),
            P(("groups", "sec"), None, None, None),
            P(("groups", "sec"), None, None, None),
        ),
        out_specs=P(("groups", "sec"), None, None),
        check_vma=False,
    )
```
